256 devices in a mesh: row: 8 (over z), col: 8 (over x, core), rep: 4 (over y).
Axes of the slice: x: 4, y: 4, z: 8, core: 2. Of those that a mesh axis runs over, the one named last changes fastest.
Arguments:
- tensor_tiles: bfloat16 [1024, 4, 128, 128], P(('row', 'col', 'rep')), may hold values from -12 to 12
- tile_pairs: int32 [1024], P(('row', 'col', 'rep')), may hold values from 0 to 3, as said below
- tile_counts: int32 [256], P(('row', 'col', 'rep')), may hold values from 1 to 4, as said below
- occupied: bfloat16 [4096, 4096], P(('col', 'rep'), 'row'), as said below
- virtual: bfloat16 [4096, 4096], P(('col', 'rep'), 'row'), as said below
Outputs:
- polar: float32 [4, 4], replicated
- dressed: bfloat16 [4096, 4, 4096], P(('col', 'rep'), None, 'row')
The draws below stay inside these ranges and needn't reach their ends.
Inputs may be any that keep to these rules, and one draw needn't show every extreme that they name: `tile_pairs`: the 4 entries of one block are distinct: a permutation of its tile pairs. `tile_counts`: some block has all 4 entries live. `occupied`: Symmetric. `virtual`: Symmetric.
All inputs are finite; a program needn't handle non-finite values.
Results may differ from the reference program's by a relative error of at most 0.0049.
Values may be sent and summed in bfloat16 or wider, within the bound.
A program may use at most 128 MiB of HBM per device.

```python
import math
import jax
import jax.numpy as jnp

TILE = 128
SPAN = 1
AUX = 4
SLOTS = 4
NAO = 4096
N_ROW = 8
N_COL = 8
N_REP = 4
DEVICES = 256


def symmetrize(entries):
    scaled = entries + entries.T
    return (scaled * 0.5 ** 0.5 / math.sqrt(NAO)).astype(jnp.bfloat16)


def draw_occupied(key, part):
    key = jax.random.fold_in(key, 11)
    base_key = jax.random.fold_in(key, 0)
    entries = jax.random.normal(base_key, (NAO, NAO), jnp.float32)
    return symmetrize(entries)


def draw_virtual(key, part):
    key = jax.random.fold_in(key, 12)
    base_key = jax.random.fold_in(key, 0)
    entries = jax.random.normal(base_key, (NAO, NAO), jnp.float32)
    return symmetrize(entries)


def draw_tile_pairs(key, part):
    key = jax.random.fold_in(key, 13)
    device_keys = jax.random.split(key, DEVICES)
    orders = jax.vmap(lambda device_key: jax.random.permutation(device_key, SLOTS))(device_keys)
    return orders.reshape(-1).astype(jnp.int32)


def draw_tile_counts(key, part):
    key = jax.random.fold_in(key, 14)
    first_key, second_key, third_key = jax.random.split(key, 3)
    first = jax.random.randint(first_key, (DEVICES,), 1, SLOTS + 1)
    second = jax.random.randint(second_key, (DEVICES,), 1, SLOTS + 1)
    fullest = jax.random.randint(third_key, (), 0, DEVICES)
    counts = jnp.where(jnp.arange(DEVICES) == fullest, SLOTS, jnp.minimum(first, second))
    return counts.astype(jnp.int32)


def level_of(rng, shape, cuts, least, top_value):
    factor_of, own = 1.0, jax.random.fold_in(rng, 6)
    for dim, blocks in cuts:
        steps = jnp.exp(jax.random.uniform(jax.random.fold_in(own, dim), (blocks,), jnp.float32, least / len(cuts), top_value / len(cuts)))
        factor_of = factor_of * jnp.repeat(steps, shape[dim] // blocks).reshape([-1 if axis == dim else 1 for axis in range(len(shape))])
    return factor_of


def centred(own_key, dims, width, reach, cuts=(), kind=jnp.bfloat16):
    loudness = level_of(own_key, dims, cuts, -0.22, 0.18) if cuts else 1.0
    values = jax.random.normal(own_key, dims, jnp.float32) * width * loudness
    return jnp.minimum(jnp.maximum(values, -reach), reach).astype(kind)


def setup_inputs(seed: int = 0) -> dict:
    seeds = jax.random.split(jax.random.key(seed), 6)
    tensor_tiles = centred(seeds[0], (DEVICES * SLOTS, AUX, TILE, TILE), 2.0, 12.0, ((0, 256),))
    tile_pairs = draw_tile_pairs(jax.random.fold_in(seeds[5], 71), 0)
    tile_counts = draw_tile_counts(jax.random.fold_in(seeds[5], 71), 0)
    occupied = draw_occupied(jax.random.fold_in(seeds[5], 71), 0)
    virtual = draw_virtual(jax.random.fold_in(seeds[5], 71), 0)
    return {"tensor_tiles": tensor_tiles, "tile_pairs": tile_pairs, "tile_counts": tile_counts, "occupied": occupied, "virtual": virtual}


def reference(tensor_tiles, tile_pairs, tile_counts, occupied, virtual):
    nu_tiles = NAO // (N_ROW * TILE)
    groups = N_COL * N_REP
    entry = jnp.arange(DEVICES * SLOTS, dtype=jnp.int32)
    block = (entry // SLOTS).astype(jnp.int32)
    live = (entry % SLOTS) < tile_counts[block]
    first_tile = (block % groups) * SPAN + tile_pairs // nu_tiles
    second_tile = (block // groups) * nu_tiles + tile_pairs % nu_tiles
    kept = jnp.where(live[:, None, None, None], tensor_tiles.astype(jnp.float32), jnp.float32(0.0))
    blocks = jnp.zeros((NAO // TILE, NAO // TILE, AUX, TILE, TILE), jnp.float32)
    blocks = blocks.at[first_tile.astype(jnp.int32), second_tile.astype(jnp.int32)].add(kept)
    tensor = blocks.transpose(2, 0, 3, 1, 4).reshape(AUX, NAO, NAO)
    half_product = jnp.einsum("pmn,ns->spm", tensor, virtual.astype(jnp.float32)).astype(jnp.bfloat16)
    dressed = jnp.einsum("lm,spm->lps", occupied.astype(jnp.float32), half_product.astype(jnp.float32)).astype(jnp.bfloat16)
    polar = jnp.einsum("pls,lqs->pq", tensor, dressed.astype(jnp.float32)) / NAO
    return polar, dressed
```

```python
import jax
import jax.numpy as jnp
from jax import lax
from jax.experimental import pallas as pl
from jax.experimental.pallas import tpu as pltpu
from jax.sharding import PartitionSpec as P

MESH = pl.DeviceIdType.MESH
F32, BF16 = jnp.float32, jnp.bfloat16
TILE, WIDTH, AUX = 128, 512, 4
NZ, NX, NY = 8, 4, 4
HALF = TILE // 2
OCC = 4


def kernel(
    tiles, pairs, counts, occ, virt, polar, dressed,
    bl, zb, vp, ob, hg, ps, pr, pf, qs, qa, qb,
    zs, zr, vs, vr, us, ur, os_, or_, ys, yr, ks, kr, xs, xr, qss, qsr,
):
    z, col, y = lax.axis_index("row"), lax.axis_index("col"), lax.axis_index("rep")
    x, core = col // 2, col % 2
    sent = []

    def at_z(d):
        return ((z + d) % NZ, col, y)

    def at_x(d):
        return (z, (col + 2 * d) % (2 * NX), y)

    def at_y(d):
        return (z, col, (y + d) % NY)

    def at_xy(dx, dy):
        return (z, (col + 2 * dx) % (2 * NX), (y + dy) % NY)

    sibling = (z, x * 2 + 1 - core, y)

    def remote(src, dst, send, recv, to):
        return pltpu.make_async_remote_copy(
            src_ref=src, dst_ref=dst, send_sem=send, recv_sem=recv, device_id=to, device_id_type=MESH
        )

    def go(copy):
        copy.start()
        sent.append(copy)

    barrier = pltpu.get_barrier_semaphore()
    partners = [at_z(d) for d in range(1, NZ)]
    partners += [at_xy(dx, dy) for dx in range(NX) for dy in range(NY) if dx or dy]
    partners += [sibling]
    for to in partners:
        pl.semaphore_signal(barrier, inc=1, device_id=to, device_id_type=MESH)

    live = counts[0]
    for q in range(4):
        where = jnp.int32(0)
        for t in range(1, 4):
            where = jnp.where(pairs[t] == q, jnp.int32(t), where)
        keep = where < live
        for p in range(AUX):
            tile = tiles[where, p]
            tile = jnp.where(keep, tile, jnp.zeros_like(tile))
            bl[p, :, q * TILE : (q + 1) * TILE] = tile
    zb[OCC, 0] = occ[...]
    for p in range(AUX):
        zb[p, 0] = bl[p]
    vp[x, core, y] = virt[...]

    pl.semaphore_wait(barrier, len(partners))

    def ring(a, k, way, sub):
        slot_from = (NZ - (k - 1)) % NZ if way == 0 else k - 1
        slot_to = NZ - k if way == 0 else k
        rows = pl.ds(sub * HALF, HALF)
        return remote(
            zb.at[a, slot_from, rows], zb.at[a, slot_to, rows],
            zs.at[a, k - 1, way, sub], zr.at[a, k - 1, way, sub], at_z(1 if way == 0 else -1),
        )

    def legs(k):
        if k == 4:
            return [(0, 0), (1, 1)]
        return [(0, 0), (1, 0), (0, 1), (1, 1)]

    def z_start(a):
        for way, sub in legs(1):
            go(ring(a, 1, way, sub))

    def z_step(a, k):
        for way, sub in legs(k):
            ring(a, k, way, sub).wait_recv()
            if k < 4 and (way, sub) in legs(k + 1):
                go(ring(a, k + 1, way, sub))

    def v_block(j):
        return (
            jnp.where(core == 0, x, (x - j + NX) % NX),
            jnp.where(core == 0, (y - j + NY) % NY, y),
        )

    def v_peer(d, first):
        on_y = jnp.where(core == 0, 1, 0) if first else jnp.where(core == 0, 0, 1)
        dx, dy = d * (1 - on_y), d * on_y
        return (z, (col + 2 * dx) % (2 * NX), (y + dy) % NY)

    def v_copy(j, d, first):
        bx, by = v_block(j)
        i = d - 1 if first else 3 + j * 3 + d - 1
        ref = vp.at[bx, core, by]
        return remote(ref, ref, vs.at[i], vr.at[i], v_peer(d, first))

    def v_landed(j, d):
        bx, by = v_block(j)
        bx = jnp.where(core == 0, (x - d + NX) % NX, bx)
        by = jnp.where(core == 0, by, (y - d + NY) % NY)
        return bx, by

    def v_swap(j, d):
        bx, by = v_landed(j, d)
        ref = vp.at[bx, core, by]
        return remote(ref, ref, us.at[j, d], ur.at[j, d], sibling)

    def v_start():
        for d in (1, 3, 2):
            go(v_copy(0, d, True))
        for d in (1, 3, 2):
            go(v_copy(0, d, False))
        go(v_swap(0, 0))

    def v_first(j):
        v_copy(0, j, True).wait_recv()
        for d in (1, 3, 2):
            go(v_copy(j, d, False))
        go(v_swap(j, 0))

    def v_second(j):
        for d in (1, 3, 2):
            v_copy(j, d, False).wait_recv()
            go(v_swap(j, d))

    def v_done():
        for j in range(4):
            for d in range(4):
                v_swap(j, d).wait_recv()

    def z_dots(a, offsets, total=None):
        for s in offsets:
            m = (z + s) % NZ
            v = vp[m // 2, m % 2].reshape(WIDTH, WIDTH)
            term = jnp.dot(zb[a, s], v, preferred_element_type=F32)
            total = term if total is None else total + term
        return total

    def o_copy(d, h):
        m = 2 * ((x + d) % NX) + h
        slot = (m - z + NZ) % NZ
        return remote(
            zb.at[OCC, slot], ob.at[h, NX - d], os_.at[d - 1, h], or_.at[d - 1, h], at_x(d)
        )

    def o_start():
        for d in (2, 1, 3):
            for h in range(2):
                go(o_copy(d, h))
        for h in range(2):
            ob[h, 0] = zb[OCC, (2 * x + h - z + NZ) % NZ]

    def o_done():
        for d in (2, 1, 3):
            for h in range(2):
                o_copy(d, h).wait_recv()

    def y_copy(p, d):
        ref = hg.at[p, core, y]
        return remote(ref, ref, ys.at[p, d - 1], yr.at[p, d - 1], at_y(d))

    def y_swap(p, j):
        ref = hg.at[p, core, (y - j + NY) % NY]
        return remote(ref, ref, ks.at[p, j], kr.at[p, j], sibling)

    def y_start(p, value):
        hg[p, core, y] = value
        for d in (2, 1, 3):
            go(y_copy(p, d))
        go(y_swap(p, 0))

    def y_done(p):
        for d in (1, 3, 2):
            y_copy(p, d).wait_recv()
            go(y_swap(p, d))

    def x_copy(p, d):
        return remote(ps.at[p, d - 1], pr.at[p, d - 1], xs.at[p, d - 1], xr.at[p, d - 1], at_x(d))

    def x_start(p):
        for j in range(4):
            y_swap(p, j).wait_recv()
        h0 = hg[p, 0].reshape(WIDTH, WIDTH)
        h1 = hg[p, 1].reshape(WIDTH, WIDTH)
        for d in (2, 1, 3):
            part = jnp.dot(ob[0, d], h0, preferred_element_type=F32)
            part += jnp.dot(ob[1, d], h1, preferred_element_type=F32)
            ps[p, d - 1] = part.astype(BF16)
            go(x_copy(p, d))
        part = jnp.dot(ob[0, 0], h0, preferred_element_type=F32)
        part += jnp.dot(ob[1, 0], h1, preferred_element_type=F32)
        pf[p] = part

    def x_done(p):
        total = pf[p]
        for d in (1, 3, 2):
            x_copy(p, d).wait_recv()
            total += pr[p, d - 1].astype(F32)
        return total.astype(BF16)

    rows = lax.broadcasted_iota(jnp.int32, (8, 128), 0)
    lanes = lax.broadcasted_iota(jnp.int32, (8, 128), 1)

    def share(q, value):
        dressed[q] = value
        mine = jnp.zeros((8, 128), F32)
        d = value.astype(F32)
        for p in range(AUX):
            s = jnp.sum(bl[p].astype(F32) * d)
            mine = jnp.where((rows == p) & (lanes == q), s, mine)
        return mine

    z_start(0)
    z_start(OCC)
    v_start()
    z_step(0, 1)
    v_first(1)
    v_first(3)
    z_step(OCC, 1)
    v_first(2)
    z_step(0, 2)
    v_second(0)
    z_step(OCC, 2)
    z_step(0, 3)
    z_start(1)
    v_second(1)
    v_second(3)
    z_step(OCC, 3)
    v_second(2)
    z_step(0, 4)
    v_done()
    y_start(0, z_dots(0, range(8)).astype(BF16))
    z_step(1, 1)
    z_start(2)
    z_step(OCC, 4)
    o_start()
    z_step(1, 2)
    z_step(2, 1)
    y_done(0)
    z_step(1, 3)
    z_step(2, 2)
    o_done()
    x_start(0)
    z_step(1, 4)
    z_start(3)
    y_start(1, z_dots(1, range(8)).astype(BF16))
    z_step(2, 3)
    z_step(3, 1)
    mine = share(0, x_done(0))
    z_step(2, 4)
    y_start(2, z_dots(2, range(8)).astype(BF16))
    y_done(1)
    z_step(3, 2)
    x_start(1)
    z_step(3, 3)
    mine += share(1, x_done(1))
    y_done(2)
    x_start(2)
    last = z_dots(3, (0, 1, 2, 3, 5, 6, 7))
    z_step(3, 4)
    y_start(3, z_dots(3, (4,), last).astype(BF16))
    mine += share(2, x_done(2))
    y_done(3)
    x_start(3)
    mine += share(3, x_done(3))

    qs[0] = mine
    swap = remote(qs.at[0], qs.at[1], qss.at[0], qsr.at[0], sibling)
    go(swap)
    swap.wait_recv()
    here = x * NY + y
    qa[here] = qs[0] + qs[1]
    plane = []
    for i in range(1, NX * NY):
        ref = qa.at[here]
        plane.append(remote(ref, ref, qss.at[i], qsr.at[i], at_xy(i // NY, i % NY)))
    for copy in plane:
        go(copy)
    for copy in plane:
        copy.wait_recv()
    qb[z] = jnp.sum(qa[...], axis=0)
    line = [remote(qb.at[z], qb.at[z], qss.at[15 + d], qsr.at[15 + d], at_z(d)) for d in range(1, NZ)]
    for copy in line:
        go(copy)
    for copy in line:
        copy.wait_recv()
    polar[...] = jnp.sum(qb[...], axis=0)
    for copy in sent:
        copy.wait_send()


def on_device(tensor_tiles, tile_pairs, tile_counts, occupied, virtual):
    vmem = pl.BlockSpec(memory_space=pltpu.VMEM)
    smem = pl.BlockSpec(memory_space=pltpu.SMEM)
    dma = pltpu.SemaphoreType.DMA
    block = (TILE, WIDTH)
    shares, dressed = pl.pallas_call(
        kernel,
        out_shape=(
            jax.ShapeDtypeStruct((8, 128), F32),
            jax.ShapeDtypeStruct((AUX, *block), BF16),
        ),
        in_specs=[vmem, smem, smem, vmem, vmem],
        out_specs=(vmem, vmem),
        scratch_shapes=[
            pltpu.VMEM((AUX, *block), BF16),
            pltpu.VMEM((AUX + 1, NZ, *block), BF16),
            pltpu.VMEM((NX, 2, NY, *block), BF16),
            pltpu.VMEM((2, NX, *block), BF16),
            pltpu.VMEM((AUX, 2, NY, *block), BF16),
            pltpu.VMEM((AUX, 3, *block), BF16),
            pltpu.VMEM((AUX, 3, *block), BF16),
            pltpu.VMEM((AUX, *block), F32),
            pltpu.VMEM((2, 8, 128), F32),
            pltpu.VMEM((16, 8, 128), F32),
            pltpu.VMEM((8, 8, 128), F32),
            dma((5, 4, 2, 2)), dma((5, 4, 2, 2)),
            dma((15,)), dma((15,)),
            dma((4, 4)), dma((4, 4)),
            dma((3, 2)), dma((3, 2)),
            dma((4, 3)), dma((4, 3)),
            dma((4, 4)), dma((4, 4)),
            dma((4, 3)), dma((4, 3)),
            dma((23,)), dma((23,)),
        ],
        compiler_params=pltpu.CompilerParams(
            collective_id=0, has_side_effects=True, vmem_limit_bytes=48 * 2**20
        ),
        cost_estimate=pl.CostEstimate(flops=4 * 2**30, bytes_accessed=2**21, transcendentals=0),
    )(tensor_tiles, tile_pairs, tile_counts, occupied, virtual)
    return shares[:AUX, :AUX] / (NZ * WIDTH), dressed.transpose(1, 0, 2)


def solution(mesh):
    spread = P(("row", "col", "rep"))
    return jax.shard_map(
        on_device,
        mesh=mesh,
        in_specs=(
            P(("row", "col", "rep"), None, None, None),
            spread,
            spread,
            P(("col", "rep"), "row"),
            P(("col", "rep"), "row"),
        ),
        out_specs=(P(), P(("col", "rep"), None, "row")),
        check_vma=False,
    )
```

```python
import jax
import jax.numpy as jnp
from jax import lax
from jax.experimental import pallas as pl
from jax.experimental.pallas import tpu as pltpu
from jax.sharding import PartitionSpec as P

MESH = pl.DeviceIdType.MESH
F32, BF16 = jnp.float32, jnp.bfloat16
TILE, WIDTH, AUX = 128, 512, 4
NZ, NX, NY = 8, 4, 4
HALF = TILE // 2
PARTS = 2
VIRT, TENSOR = 0, 1
OCC = 4


def kernel(
    tiles_in, pairs_in, counts_in, occ, virt, polar, dressed,
    tiles, pairs, counts, bl, bx, zb, vp, ob, hg, ps, pr, pf, dv, qs, qa, qb,
    zs, zr, vs, vr, us, ur, os_, or_, bs, br, ys, yr, ks, kr, xs, xr, qss, qsr, ins, outs,
):
    z, col, y = lax.axis_index("row"), lax.axis_index("col"), lax.axis_index("rep")
    x, core = col // 2, col % 2
    sent = []

    def at_z(d):
        return ((z + d) % NZ, col, y)

    def at_x(d):
        return at_xy(d, 0)

    def at_y(d):
        return at_xy(0, d)

    def at_xy(dx, dy):
        return (z, (col + 2 * dx) % (2 * NX), (y + dy) % NY)

    sibling = (z, x * 2 + 1 - core, y)

    def remote(src, dst, send, recv, to):
        return pltpu.make_async_remote_copy(
            src_ref=src, dst_ref=dst, send_sem=send, recv_sem=recv, device_id=to, device_id_type=MESH
        )

    def go(copy):
        copy.start()
        sent.append(copy)

    loads = [
        pltpu.make_async_copy(src, dst, ins.at[i])
        for i, (src, dst) in enumerate([
            (pairs_in, pairs), (counts_in, counts), (tiles_in, tiles),
            (occ, zb.at[OCC, 0]), (virt, vp.at[VIRT, x, core, y]),
        ])
    ]
    for load in loads:
        load.start()

    barrier = pltpu.get_barrier_semaphore()
    partners = [sibling] + [at_z(d) for d in range(1, NZ)]
    partners += [at_xy(dx, dy) for dx in range(NX) for dy in range(NY) if dx or dy]
    for to in partners:
        pl.semaphore_signal(barrier, inc=1, device_id=to, device_id_type=MESH)

    for load in loads:
        load.wait()

    live = counts[0]
    for q in range(4):
        where = jnp.int32(0)
        for t in range(1, 4):
            where = jnp.where(pairs[t] == q, jnp.int32(t), where)
        keep = where < live
        for p in range(AUX):
            tile = tiles[where, p]
            tile = jnp.where(keep, tile, jnp.zeros_like(tile))
            bl[p, :, q * TILE : (q + 1) * TILE] = tile
    for p in range(AUX):
        zb[p, 0] = bl[p]
    vp[TENSOR, x, core, y] = bl[AUX - 1]

    pl.semaphore_wait(barrier, len(partners))

    def ring(a, k, way, sub):
        slot_from = (NZ - (k - 1)) % NZ if way == 0 else k - 1
        slot_to = NZ - k if way == 0 else k
        rows = pl.ds(sub * (TILE // PARTS), TILE // PARTS)
        return remote(
            zb.at[a, slot_from, rows], zb.at[a, slot_to, rows],
            zs.at[a, k - 1, way, sub], zr.at[a, k - 1, way, sub], at_z(1 if way == 0 else -1),
        )

    def ways(k, sub):
        if k == 4:
            return [0] if sub < PARTS // 2 else [1]
        return [0, 1]

    def z_start(a):
        for sub in range(PARTS):
            for way in (0, 1):
                go(ring(a, 1, way, sub))

    def z_sub(a, k, sub):
        for way in (0, 1):
            ring(a, k, way, sub).wait_recv()
            if way in ways(k + 1, sub):
                go(ring(a, k + 1, way, sub))

    def z_last(a):
        for sub in range(PARTS):
            ring(a, 4, ways(4, sub)[0], sub).wait_recv()

    def block_at(j, d):
        return (x - j + NX) % NX, core, (y - d + NY) % NY

    def panel_peer(d, first):
        return at_x(d) if first else at_y(d)

    def p_send(b, j, d):
        ref = vp.at[b, *block_at(0 if j is None else j, 0)]
        i = 0 if j is None else 1 + j
        return remote(ref, ref, vs.at[b, i, 0, d // 2], vr.at[b, i, 0, d // 2], panel_peer(d, j is None))

    def p_pass(b, j, d):
        bx, bc, by = block_at(d, 0) if j is None else block_at(j, d)
        ref = vp.at[b, bx, bc, by, pl.ds(HALF * (d // 2), HALF)]
        i = 0 if j is None else 1 + j
        return remote(ref, ref, vs.at[b, i, 1, d // 2], vr.at[b, i, 1, d // 2], panel_peer(d, j is None))

    def p_swap(b, j, d):
        ref = vp.at[b, *block_at(j, d)]
        return remote(ref, ref, us.at[b, j, d], ur.at[b, j, d], sibling)

    def p_out(b, j):
        for d in (1, 3):
            go(p_send(b, j, d))
        go(p_swap(b, j, 0))

    def p_start(b):
        for d in (1, 3):
            go(p_send(b, None, d))
        p_out(b, 0)

    def p_first(b):
        for d in (1, 3):
            p_send(b, None, d).wait_recv()
            go(p_pass(b, None, d))
        for d in (1, 3):
            p_out(b, d)

    def p_first_far(b):
        for d in (1, 3):
            p_pass(b, None, d).wait_recv()
        p_out(b, 2)

    def p_second(b, j):
        for d in (1, 3):
            p_send(b, j, d).wait_recv()
            go(p_pass(b, j, d))
            go(p_swap(b, j, d))

    def p_second_far(b, j):
        for d in (1, 3):
            p_pass(b, j, d).wait_recv()
        go(p_swap(b, j, 2))

    def p_done(b):
        for j in range(4):
            for d in range(4):
                p_swap(b, j, d).wait_recv()

    def z_dots(a, offsets, b, total=None):
        for s in offsets:
            m = (z + s) % NZ
            v = vp[b, m // 2, m % 2].reshape(WIDTH, WIDTH)
            term = jnp.dot(zb[a, s], v, preferred_element_type=F32)
            total = term if total is None else total + term
        return total

    def o_copy(d, h):
        m = 2 * ((x + d) % NX) + h
        slot = (m - z + NZ) % NZ
        return remote(
            zb.at[OCC, slot], ob.at[h, NX - d], os_.at[d - 1, h], or_.at[d - 1, h], at_x(d)
        )

    def o_arrived(slot):
        m = (z + slot) % NZ
        d, h = (m // 2 - x + NX) % NX, m % 2

        @pl.when(d == 0)
        def _():
            ob[h, 0] = zb[OCC, slot]

        @pl.when(d != 0)
        def _():
            remote(
                zb.at[OCC, slot], ob.at[h, NX - d], os_.at[d - 1, h], or_.at[d - 1, h], at_x(d)
            ).start()

    def o_done():
        for d in (1, 2, 3):
            for h in range(2):
                o_copy(d, h).wait_recv()

    rows = lax.broadcasted_iota(jnp.int32, (8, 128), 0)
    lanes = lax.broadcasted_iota(jnp.int32, (8, 128), 1)

    def place(p, q):
        return (rows == p) & (lanes == q)

    def y_copy(p, d):
        ref = hg.at[p, core, y]
        return remote(ref, ref, ys.at[p, d - 1], yr.at[p, d - 1], at_y(d))

    def y_swap(p, j):
        ref = hg.at[p, core, (y - j + NY) % NY]
        return remote(ref, ref, ks.at[p, j], kr.at[p, j], sibling)

    def y_start(p, value):
        hg[p, core, y] = value
        for d in (2, 1, 3):
            go(y_copy(p, d))
        go(y_swap(p, 0))

    def y_done(p):
        for d in (1, 3, 2):
            y_copy(p, d).wait_recv()
            go(y_swap(p, d))

    def x_copy(p, d):
        return remote(ps.at[p, d - 1], pr.at[p, d - 1], xs.at[p, d - 1], xr.at[p, d - 1], at_x(d))

    def b_copy(d):
        return remote(bl, bx.at[NX - d], bs.at[d - 1], br.at[d - 1], at_x(d))

    def b_start():
        for d in (2, 1, 3):
            go(b_copy(d))

    def b_done():
        for d in (1, 3, 2):
            b_copy(d).wait_recv()

    def x_start(p):
        for j in range(4):
            y_swap(p, j).wait_recv()
        h0 = hg[p, 0].reshape(WIDTH, WIDTH)
        h1 = hg[p, 1].reshape(WIDTH, WIDTH)
        for d in (2, 1, 3, 0):
            part = jnp.dot(ob[0, d], h0, preferred_element_type=F32)
            part += jnp.dot(ob[1, d], h1, preferred_element_type=F32)
            pf[p, d] = part
            if d:
                ps[p, d - 1] = part.astype(BF16)
                go(x_copy(p, d))

    def x_share(q):
        mine = jnp.zeros((8, 128), F32)
        for p in range(AUX):
            total = jnp.sum(bl[p].astype(F32) * pf[q, 0], axis=0)
            for d in (1, 2, 3):
                total += jnp.sum(bx[d, p].astype(F32) * pf[q, d], axis=0)
            mine = jnp.where(place(p, q), jnp.sum(total), mine)
        return mine

    def x_done(p):
        total = pf[p, 0]
        for d in (1, 3, 2):
            x_copy(p, d).wait_recv()
            total += pr[p, d - 1].astype(F32)
        return total

    def put(q):
        return pltpu.make_async_copy(dv.at[q], dressed.at[q], outs.at[q])

    def dot_all(left, right):
        return jnp.sum(left.astype(F32) * right.astype(F32))

    def out(q, total):
        value = total.astype(BF16)
        dv[q] = value
        put(q).start()

    def d_share(q, total):
        mine = jnp.zeros((8, 128), F32)
        for p in range(AUX):
            mine = jnp.where(place(p, q), dot_all(bl[p], total), mine)
        return mine

    def q_copies(stage):
        if stage == 0:
            buffer, mine, peers, base = qs, core, [sibling], 0
        elif stage == 1:
            buffer, mine, peers, base = qa, z, [at_z(i) for i in range(1, NZ)], 1
        else:
            buffer, mine, base = qb, x * NY + y, 8
            peers = [at_xy(i // NY, i % NY) for i in range(1, NX * NY)]
        ref = buffer.at[mine]
        return buffer, mine, [
            remote(ref, ref, qss.at[base + i], qsr.at[base + i], to) for i, to in enumerate(peers)
        ]

    def q_start(stage, value):
        buffer, mine, copies = q_copies(stage)
        buffer[mine] = value
        for copy in copies:
            go(copy)

    def q_done(stage):
        buffer, _, copies = q_copies(stage)
        for copy in copies:
            copy.wait_recv()
        return jnp.sum(buffer[...], axis=0)

    shares = []
    z_start(0)
    p_start(0)
    p_start(1)
    z_sub(0, 1, 0)
    z_sub(0, 1, 1)
    z_start(OCC)
    p_first(0)
    o_arrived(0)
    p_second(0, 0)
    z_sub(0, 2, 0)
    p_first(1)
    p_second(1, 0)
    z_sub(0, 2, 1)
    z_start(1)
    p_first_far(0)
    z_sub(OCC, 1, 0)
    p_second(0, 1)
    z_sub(OCC, 1, 1)
    o_arrived(7)
    o_arrived(1)
    p_first_far(1)
    z_sub(0, 3, 0)
    p_second(0, 3)
    z_sub(0, 3, 1)
    p_second_far(0, 0)
    z_sub(1, 1, 0)
    z_sub(1, 1, 1)
    p_second(1, 1)
    z_sub(OCC, 2, 0)
    z_sub(OCC, 2, 1)
    o_arrived(6)
    o_arrived(2)
    b_start()
    p_second(1, 3)
    z_last(0)
    z_start(2)
    p_second_far(1, 0)
    z_sub(1, 2, 0)
    z_sub(1, 2, 1)
    p_second(0, 2)
    z_sub(OCC, 3, 0)
    p_second_far(0, 1)
    z_sub(OCC, 3, 1)
    o_arrived(5)
    o_arrived(3)
    z_sub(2, 1, 0)
    p_second(1, 2)
    z_sub(2, 1, 1)
    p_second_far(0, 3)
    z_sub(1, 3, 0)
    p_second_far(1, 1)
    z_sub(1, 3, 1)
    p_second_far(1, 3)
    z_last(OCC)
    o_arrived(4)
    p_second_far(0, 2)
    z_sub(2, 2, 0)
    p_done(0)
    y_start(0, z_dots(0, range(NZ), VIRT).astype(BF16))
    z_sub(2, 2, 1)
    p_second_far(1, 2)
    z_last(1)
    y_start(1, z_dots(1, range(NZ), VIRT).astype(BF16))
    p_done(1)
    zb[3, 0] = z_dots(OCC, range(NZ), TENSOR).astype(BF16)
    z_start(3)
    z_sub(2, 3, 0)
    z_sub(2, 3, 1)
    z_sub(3, 1, 0)
    y_done(0)
    z_sub(3, 1, 1)
    z_last(2)
    y_start(2, z_dots(2, range(NZ), VIRT).astype(BF16))
    b_done()
    z_sub(3, 2, 0)
    z_sub(3, 2, 1)
    y_done(1)
    o_done()
    x_start(0)
    z_sub(3, 3, 0)
    x_start(1)
    z_sub(3, 3, 1)
    shares.append(x_share(0))
    y_done(2)
    shares.append(x_share(1))
    acc3 = z_dots(3, (0, 7, 1, 6, 2, 5, 3), VIRT)
    x_start(2)
    z_last(3)
    d3 = z_dots(3, (4,), VIRT, acc3)
    shares.append(d_share(3, d3))
    shares.append(x_share(2))
    q_start(0, shares[0] + shares[1] + shares[2] + shares[3])
    out(0, x_done(0))
    out(3, d3)
    q_start(1, q_done(0))
    out(1, x_done(1))
    q_start(2, q_done(1))
    out(2, x_done(2))
    polar[...] = q_done(2)
    for d in (1, 2, 3):
        for h in range(2):
            o_copy(d, h).wait_send()
    for copy in sent:
        copy.wait_send()
    for q in range(AUX):
        put(q).wait()


def on_device(tensor_tiles, tile_pairs, tile_counts, occupied, virtual):
    vmem = pl.BlockSpec(memory_space=pltpu.VMEM)
    hbm = pl.BlockSpec(memory_space=pl.ANY)
    dma = pltpu.SemaphoreType.DMA
    block = (TILE, WIDTH)
    shares, dressed = pl.pallas_call(
        kernel,
        out_shape=(
            jax.ShapeDtypeStruct((8, 128), F32),
            jax.ShapeDtypeStruct((AUX, *block), BF16),
        ),
        in_specs=[hbm] * 5,
        out_specs=(vmem, hbm),
        scratch_shapes=[
            pltpu.VMEM((4, AUX, TILE, TILE), BF16),
            pltpu.SMEM((4,), jnp.int32),
            pltpu.SMEM((1,), jnp.int32),
            pltpu.VMEM((AUX, *block), BF16),
            pltpu.VMEM((NX, AUX, *block), BF16),
            pltpu.VMEM((AUX + 1, NZ, *block), BF16),
            pltpu.VMEM((2, NX, 2, NY, *block), BF16),
            pltpu.VMEM((2, NX, *block), BF16),
            pltpu.VMEM((AUX, 2, NY, *block), BF16),
            pltpu.VMEM((AUX, 3, *block), BF16),
            pltpu.VMEM((AUX, 3, *block), BF16),
            pltpu.VMEM((AUX, NX, *block), F32),
            pltpu.VMEM((AUX, *block), BF16),
            pltpu.VMEM((2, 8, 128), F32),
            pltpu.VMEM((NZ, 8, 128), F32),
            pltpu.VMEM((NX * NY, 8, 128), F32),
            dma((5, 4, 2, PARTS)), dma((5, 4, 2, PARTS)),
            dma((2, 5, 2, 2)), dma((2, 5, 2, 2)),
            dma((2, 4, 4)), dma((2, 4, 4)),
            dma((3, 2)), dma((3, 2)),
            dma((3,)), dma((3,)),
            dma((4, 3)), dma((4, 3)),
            dma((4, 4)), dma((4, 4)),
            dma((4, 3)), dma((4, 3)),
            dma((23,)), dma((23,)), dma((5,)), dma((4,)),
        ],
        compiler_params=pltpu.CompilerParams(
            collective_id=0, has_side_effects=True, vmem_limit_bytes=56 * 2**20
        ),
        cost_estimate=pl.CostEstimate(flops=4 * 2**30, bytes_accessed=2**21, transcendentals=0),
    )(tensor_tiles, tile_pairs, tile_counts, occupied, virtual)
    return shares[:AUX, :AUX] / (NZ * WIDTH), dressed.transpose(1, 0, 2)


def solution(mesh):
    spread = P(("row", "col", "rep"))
    return jax.shard_map(
        on_device,
        mesh=mesh,
        in_specs=(
            P(("row", "col", "rep"), None, None, None),
            spread,
            spread,
            P(("col", "rep"), "row"),
            P(("col", "rep"), "row"),
        ),
        out_specs=(P(), P(("col", "rep"), None, "row")),
        check_vma=False,
    )
```

```python
import jax
import jax.numpy as jnp
from jax import lax
from jax.experimental import pallas as pl
from jax.experimental.pallas import tpu as pltpu
from jax.sharding import PartitionSpec as P

MESH = pl.DeviceIdType.MESH
F32, BF16 = jnp.float32, jnp.bfloat16
TILE, WIDTH, AUX = 128, 512, 4
NZ, NX, NY = 8, 4, 4
HALF = TILE // 2
PARTS = 2
VIRT, TENSOR = 0, 1
OCC = 4


def kernel(
    tiles_in, pairs_in, counts_in, occ, virt, polar, dressed,
    tiles, pairs, counts, bl, bx, zb, vp, ob, hg, ps, pr, pf, dv, qs, qa, qb,
    zs, zr, vs, vr, us, ur, os_, or_, bs, br, ys, yr, ks, kr, xs, xr, qss, qsr, ins, outs,
):
    z, col, y = lax.axis_index("row"), lax.axis_index("col"), lax.axis_index("rep")
    x, core = col // 2, col % 2
    sent = []

    def at_z(d):
        return ((z + d) % NZ, col, y)

    def at_x(d):
        return at_xy(d, 0)

    def at_y(d):
        return at_xy(0, d)

    def at_xy(dx, dy):
        return (z, (col + 2 * dx) % (2 * NX), (y + dy) % NY)

    sibling = (z, x * 2 + 1 - core, y)

    def remote(src, dst, send, recv, to):
        return pltpu.make_async_remote_copy(
            src_ref=src, dst_ref=dst, send_sem=send, recv_sem=recv, device_id=to, device_id_type=MESH
        )

    def go(copy):
        copy.start()
        sent.append(copy)

    loads = [
        pltpu.make_async_copy(src, dst, ins.at[i])
        for i, (src, dst) in enumerate([
            (pairs_in, pairs), (counts_in, counts), (tiles_in, tiles),
            (occ, zb.at[OCC, 0]), (virt, vp.at[VIRT, x, core, y]),
        ])
    ]
    for load in loads:
        load.start()

    barrier = pltpu.get_barrier_semaphore()
    partners = [sibling] + [at_z(d) for d in range(1, NZ)]
    partners += [at_xy(dx, dy) for dx in range(NX) for dy in range(NY) if dx or dy]
    for to in partners:
        pl.semaphore_signal(barrier, inc=1, device_id=to, device_id_type=MESH)

    for load in loads:
        load.wait()

    live = counts[0]
    for q in range(4):
        where = jnp.int32(0)
        for t in range(1, 4):
            where = jnp.where(pairs[t] == q, jnp.int32(t), where)
        keep = where < live
        for p in range(AUX):
            tile = tiles[where, p]
            tile = jnp.where(keep, tile, jnp.zeros_like(tile))
            bl[p, :, q * TILE : (q + 1) * TILE] = tile
    for p in range(AUX):
        zb[p, 0] = bl[p]
    vp[TENSOR, x, core, y] = bl[AUX - 1]

    pl.semaphore_wait(barrier, len(partners))

    def ring(a, k, way, sub):
        slot_from = (NZ - (k - 1)) % NZ if way == 0 else k - 1
        slot_to = NZ - k if way == 0 else k
        rows = pl.ds(sub * (TILE // PARTS), TILE // PARTS)
        return remote(
            zb.at[a, slot_from, rows], zb.at[a, slot_to, rows],
            zs.at[a, k - 1, way, sub], zr.at[a, k - 1, way, sub], at_z(1 if way == 0 else -1),
        )

    def ways(k, sub):
        if k == 4:
            return [0] if sub < PARTS // 2 else [1]
        return [0, 1]

    def z_start(a):
        for sub in range(PARTS):
            for way in (0, 1):
                go(ring(a, 1, way, sub))

    def z_sub(a, k, sub):
        for way in (0, 1):
            ring(a, k, way, sub).wait_recv()
            if way in ways(k + 1, sub):
                go(ring(a, k + 1, way, sub))

    def z_last(a):
        for sub in range(PARTS):
            ring(a, 4, ways(4, sub)[0], sub).wait_recv()

    def block_at(j, d):
        return (x - j + NX) % NX, core, (y - d + NY) % NY

    def panel_peer(d, first):
        return at_x(d) if first else at_y(d)

    def p_send(b, j, d):
        ref = vp.at[b, *block_at(0 if j is None else j, 0)]
        i = 0 if j is None else 1 + j
        return remote(ref, ref, vs.at[b, i, 0, d // 2], vr.at[b, i, 0, d // 2], panel_peer(d, j is None))

    def p_pass(b, j, d):
        bx, bc, by = block_at(d, 0) if j is None else block_at(j, d)
        ref = vp.at[b, bx, bc, by, pl.ds(HALF * (d // 2), HALF)]
        i = 0 if j is None else 1 + j
        return remote(ref, ref, vs.at[b, i, 1, d // 2], vr.at[b, i, 1, d // 2], panel_peer(d, j is None))

    def p_swap(b, j, d):
        ref = vp.at[b, *block_at(j, d)]
        return remote(ref, ref, us.at[b, j, d], ur.at[b, j, d], sibling)

    def p_out(b, j):
        for d in (1, 3):
            go(p_send(b, j, d))
        go(p_swap(b, j, 0))

    def p_start(b):
        for d in (1, 3):
            go(p_send(b, None, d))
        p_out(b, 0)

    def p_first(b):
        for d in (1, 3):
            p_send(b, None, d).wait_recv()
            go(p_pass(b, None, d))
        for d in (1, 3):
            p_out(b, d)

    def p_first_far(b):
        for d in (1, 3):
            p_pass(b, None, d).wait_recv()
        p_out(b, 2)

    def p_second(b, j):
        for d in (1, 3):
            p_send(b, j, d).wait_recv()
            go(p_pass(b, j, d))
            go(p_swap(b, j, d))

    def p_second_far(b, j):
        for d in (1, 3):
            p_pass(b, j, d).wait_recv()
        go(p_swap(b, j, 2))

    def p_done(b):
        for j in range(4):
            for d in range(4):
                p_swap(b, j, d).wait_recv()

    def z_dots(a, offsets, b, total=None):
        for s in offsets:
            m = (z + s) % NZ
            v = vp[b, m // 2, m % 2].reshape(WIDTH, WIDTH)
            term = jnp.dot(zb[a, s], v, preferred_element_type=F32)
            total = term if total is None else total + term
        return total

    def o_copy(d, h):
        m = 2 * ((x + d) % NX) + h
        slot = (m - z + NZ) % NZ
        return remote(
            zb.at[OCC, slot], ob.at[h, NX - d], os_.at[d - 1, h], or_.at[d - 1, h], at_x(d)
        )

    def o_arrived(slot):
        m = (z + slot) % NZ
        d, h = (m // 2 - x + NX) % NX, m % 2

        @pl.when(d == 0)
        def _():
            ob[h, 0] = zb[OCC, slot]

        @pl.when(d != 0)
        def _():
            remote(
                zb.at[OCC, slot], ob.at[h, NX - d], os_.at[d - 1, h], or_.at[d - 1, h], at_x(d)
            ).start()

    def o_done():
        for d in (1, 2, 3):
            for h in range(2):
                o_copy(d, h).wait_recv()

    rows = lax.broadcasted_iota(jnp.int32, (8, 128), 0)
    lanes = lax.broadcasted_iota(jnp.int32, (8, 128), 1)

    def place(p, q):
        return (rows == p) & (lanes == q)

    def y_copy(p, d):
        ref = hg.at[p, core, y]
        return remote(ref, ref, ys.at[p, d - 1], yr.at[p, d - 1], at_y(d))

    def y_swap(p, j):
        ref = hg.at[p, core, (y - j + NY) % NY]
        return remote(ref, ref, ks.at[p, j], kr.at[p, j], sibling)

    def y_start(p, value):
        hg[p, core, y] = value
        for d in (2, 1, 3):
            go(y_copy(p, d))
        go(y_swap(p, 0))

    def y_done(p):
        for d in (1, 3, 2):
            y_copy(p, d).wait_recv()
            go(y_swap(p, d))

    def x_copy(p, d):
        return remote(ps.at[p, d - 1], pr.at[p, d - 1], xs.at[p, d - 1], xr.at[p, d - 1], at_x(d))

    def b_copy(d):
        return remote(bl, bx.at[NX - d], bs.at[d - 1], br.at[d - 1], at_x(d))

    def b_start():
        for d in (2, 1, 3):
            go(b_copy(d))

    def b_done():
        for d in (1, 3, 2):
            b_copy(d).wait_recv()

    def x_start(p):
        for j in range(4):
            y_swap(p, j).wait_recv()
        h0 = hg[p, 0].reshape(WIDTH, WIDTH)
        h1 = hg[p, 1].reshape(WIDTH, WIDTH)
        for d in (2, 1, 3, 0):
            part = jnp.dot(ob[0, d], h0, preferred_element_type=F32)
            part += jnp.dot(ob[1, d], h1, preferred_element_type=F32)
            pf[p, d] = part
            if d:
                ps[p, d - 1] = part.astype(BF16)
                go(x_copy(p, d))

    def x_share(q):
        mine = jnp.zeros((8, 128), F32)
        for p in range(AUX):
            total = jnp.sum(bl[p].astype(F32) * pf[q, 0], axis=0)
            for d in (1, 2, 3):
                total += jnp.sum(bx[d, p].astype(F32) * pf[q, d], axis=0)
            mine = jnp.where(place(p, q), jnp.sum(total), mine)
        return mine

    def x_done(p):
        total = pf[p, 0]
        for d in (1, 3, 2):
            x_copy(p, d).wait_recv()
            total += pr[p, d - 1].astype(F32)
        return total

    def put(q):
        return pltpu.make_async_copy(dv.at[q], dressed.at[q], outs.at[q])

    def dot_all(left, right):
        return jnp.sum(left.astype(F32) * right.astype(F32))

    def out(q, total):
        value = total.astype(BF16)
        dv[q] = value
        put(q).start()

    def d_share(q, total):
        mine = jnp.zeros((8, 128), F32)
        for p in range(AUX):
            mine = jnp.where(place(p, q), dot_all(bl[p], total), mine)
        return mine

    def q_copies(stage):
        if stage == 0:
            buffer, mine, peers, base = qs, core, [sibling], 0
        elif stage == 1:
            buffer, mine, peers, base = qa, z, [at_z(i) for i in range(1, NZ)], 1
        else:
            buffer, mine, base = qb, x * NY + y, 8
            peers = [at_xy(i // NY, i % NY) for i in range(1, NX * NY)]
        ref = buffer.at[mine]
        return buffer, mine, [
            remote(ref, ref, qss.at[base + i], qsr.at[base + i], to) for i, to in enumerate(peers)
        ]

    def q_start(stage, value):
        buffer, mine, copies = q_copies(stage)
        buffer[mine] = value
        for copy in copies:
            go(copy)

    def q_done(stage):
        buffer, _, copies = q_copies(stage)
        for copy in copies:
            copy.wait_recv()
        return jnp.sum(buffer[...], axis=0)

    shares = []
    z_start(1)
    p_start(0)
    z_start(0)
    z_start(OCC)
    p_start(1)
    p_second(0, 0)
    z_sub(1, 1, 1)
    z_start(2)
    p_first(0)
    p_first(1)
    b_start()
    p_second_far(0, 0)
    z_sub(0, 1, 1)
    z_sub(OCC, 1, 0)
    z_sub(1, 2, 1)
    z_sub(OCC, 1, 1)
    p_second(1, 0)
    z_sub(OCC, 2, 0)
    p_first_far(0)
    z_sub(2, 1, 1)
    z_sub(OCC, 2, 1)
    o_arrived(1)
    z_sub(1, 1, 0)
    p_second(0, 3)
    z_sub(2, 1, 0)
    z_sub(0, 1, 0)
    p_first_far(1)
    z_sub(OCC, 3, 0)
    z_sub(OCC, 3, 1)
    p_second(0, 1)
    z_sub(1, 2, 0)
    p_second_far(0, 3)
    o_arrived(3)
    p_second(0, 2)
    p_second_far(1, 0)
    z_sub(0, 2, 1)
    o_arrived(0)
    p_second(1, 1)
    z_sub(0, 2, 0)
    p_second(1, 2)
    z_sub(1, 3, 0)
    z_last(OCC)
    z_sub(1, 3, 1)
    p_second_far(0, 1)
    p_second(1, 3)
    o_arrived(4)
    z_sub(2, 2, 1)
    o_arrived(2)
    p_second_far(0, 2)
    p_done(0)
    o_arrived(5)
    p_second_far(1, 2)
    o_arrived(7)
    z_sub(2, 2, 0)
    z_sub(0, 3, 0)
    z_last(1)
    p_second_far(1, 1)
    y_start(1, z_dots(1, range(NZ), VIRT).astype(BF16))
    z_sub(0, 3, 1)
    p_second_far(1, 3)
    p_done(1)
    z_sub(2, 3, 1)
    z_sub(2, 3, 0)
    o_arrived(6)
    zb[3, 0] = z_dots(OCC, range(NZ), TENSOR).astype(BF16)
    z_start(3)
    z_last(0)
    y_start(0, z_dots(0, range(NZ), VIRT).astype(BF16))
    b_done()
    o_done()
    y_done(1)
    z_last(2)
    z_sub(3, 1, 0)
    y_start(2, z_dots(2, range(NZ), VIRT).astype(BF16))
    z_sub(3, 1, 1)
    x_start(1)
    z_sub(3, 2, 0)
    y_done(0)
    z_sub(3, 2, 1)
    x_start(0)
    shares.append(x_share(1))
    z_sub(3, 3, 0)
    z_sub(3, 3, 1)
    y_done(2)
    acc3 = z_dots(3, (0, 7, 1, 6, 2, 5, 3), VIRT)
    shares.append(x_share(0))
    x_start(2)
    shares.append(x_share(2))
    z_last(3)
    d3 = z_dots(3, (4,), VIRT, acc3)
    shares.append(d_share(3, d3))
    q_start(0, shares[0] + shares[1] + shares[2] + shares[3])
    q_start(1, q_done(0))
    out(1, x_done(1))
    out(3, d3)
    q_start(2, q_done(1))
    out(0, x_done(0))
    out(2, x_done(2))
    polar[...] = q_done(2)
    for d in (1, 2, 3):
        for h in range(2):
            o_copy(d, h).wait_send()
    for copy in sent:
        copy.wait_send()
    for q in range(AUX):
        put(q).wait()


def on_device(tensor_tiles, tile_pairs, tile_counts, occupied, virtual):
    vmem = pl.BlockSpec(memory_space=pltpu.VMEM)
    hbm = pl.BlockSpec(memory_space=pl.ANY)
    dma = pltpu.SemaphoreType.DMA
    block = (TILE, WIDTH)
    shares, dressed = pl.pallas_call(
        kernel,
        out_shape=(
            jax.ShapeDtypeStruct((8, 128), F32),
            jax.ShapeDtypeStruct((AUX, *block), BF16),
        ),
        in_specs=[hbm] * 5,
        out_specs=(vmem, hbm),
        scratch_shapes=[
            pltpu.VMEM((4, AUX, TILE, TILE), BF16),
            pltpu.SMEM((4,), jnp.int32),
            pltpu.SMEM((1,), jnp.int32),
            pltpu.VMEM((AUX, *block), BF16),
            pltpu.VMEM((NX, AUX, *block), BF16),
            pltpu.VMEM((AUX + 1, NZ, *block), BF16),
            pltpu.VMEM((2, NX, 2, NY, *block), BF16),
            pltpu.VMEM((2, NX, *block), BF16),
            pltpu.VMEM((AUX, 2, NY, *block), BF16),
            pltpu.VMEM((AUX, 3, *block), BF16),
            pltpu.VMEM((AUX, 3, *block), BF16),
            pltpu.VMEM((AUX, NX, *block), F32),
            pltpu.VMEM((AUX, *block), BF16),
            pltpu.VMEM((2, 8, 128), F32),
            pltpu.VMEM((NZ, 8, 128), F32),
            pltpu.VMEM((NX * NY, 8, 128), F32),
            dma((5, 4, 2, PARTS)), dma((5, 4, 2, PARTS)),
            dma((2, 5, 2, 2)), dma((2, 5, 2, 2)),
            dma((2, 4, 4)), dma((2, 4, 4)),
            dma((3, 2)), dma((3, 2)),
            dma((3,)), dma((3,)),
            dma((4, 3)), dma((4, 3)),
            dma((4, 4)), dma((4, 4)),
            dma((4, 3)), dma((4, 3)),
            dma((23,)), dma((23,)), dma((5,)), dma((4,)),
        ],
        compiler_params=pltpu.CompilerParams(
            collective_id=0, has_side_effects=True, vmem_limit_bytes=56 * 2**20
        ),
        cost_estimate=pl.CostEstimate(flops=4 * 2**30, bytes_accessed=2**21, transcendentals=0),
    )(tensor_tiles, tile_pairs, tile_counts, occupied, virtual)
    return shares[:AUX, :AUX] / (NZ * WIDTH), dressed.transpose(1, 0, 2)


def solution(mesh):
    spread = P(("row", "col", "rep"))
    return jax.shard_map(
        on_device,
        mesh=mesh,
        in_specs=(
            P(("row", "col", "rep"), None, None, None),
            spread,
            spread,
            P(("col", "rep"), "row"),
            P(("col", "rep"), "row"),
        ),
        out_specs=(P(), P(("col", "rep"), None, "row")),
        check_vma=False,
    )
```

```python
import jax
import jax.numpy as jnp
from jax import lax
from jax.experimental import pallas as pl
from jax.experimental.pallas import tpu as pltpu
from jax.sharding import PartitionSpec as P

MESH = pl.DeviceIdType.MESH
F32, BF16 = jnp.float32, jnp.bfloat16
TILE, WIDTH, AUX = 128, 512, 4
NZ, NX, NY = 8, 4, 4
HALF = TILE // 2
PARTS = 2
VIRT, TENSOR = 0, 1
OCC = 4


def kernel(
    tiles_in, pairs_in, counts_in, occ, virt, polar, dressed,
    tiles, pairs, counts, bl, bx, zb, vp, ob, hg, ps, pr, pf, dv, qs, qa, qb,
    zs, zr, vs, vr, us, ur, os_, or_, bs, br, ys, yr, ks, kr, xs, xr, qss, qsr, ins, outs,
):
    z, col, y = lax.axis_index("row"), lax.axis_index("col"), lax.axis_index("rep")
    x, core = col // 2, col % 2
    sent = []

    def at_z(d):
        return ((z + d) % NZ, col, y)

    def at_x(d):
        return at_xy(d, 0)

    def at_y(d):
        return at_xy(0, d)

    def at_xy(dx, dy):
        return (z, (col + 2 * dx) % (2 * NX), (y + dy) % NY)

    sibling = (z, x * 2 + 1 - core, y)

    def remote(src, dst, send, recv, to):
        return pltpu.make_async_remote_copy(
            src_ref=src, dst_ref=dst, send_sem=send, recv_sem=recv, device_id=to, device_id_type=MESH
        )

    def go(copy):
        copy.start()
        sent.append(copy)

    loads = [
        pltpu.make_async_copy(src, dst, ins.at[i])
        for i, (src, dst) in enumerate([
            (pairs_in, pairs), (counts_in, counts), (tiles_in, tiles),
            (occ, zb.at[OCC, 0]), (virt, vp.at[VIRT, x, core, y]),
        ])
    ]
    for load in loads:
        load.start()

    barrier = pltpu.get_barrier_semaphore()
    partners = [sibling, at_z(1), at_z(-1)] + [at_xy(d, 0) for d in (1, 2, 3)] + [at_xy(0, d) for d in (1, 2, 3)]
    for to in partners:
        pl.semaphore_signal(barrier, inc=1, device_id=to, device_id_type=MESH)

    for load in loads:
        load.wait()

    live = counts[0]
    for q in range(4):
        where = jnp.int32(0)
        for t in range(1, 4):
            where = jnp.where(pairs[t] == q, jnp.int32(t), where)
        keep = where < live
        for p in range(AUX):
            tile = tiles[where, p]
            tile = jnp.where(keep, tile, jnp.zeros_like(tile))
            bl[p, :, q * TILE : (q + 1) * TILE] = tile
    for p in range(AUX):
        zb[p, 0] = bl[p]
    vp[TENSOR, x, core, y] = bl[AUX - 1]

    pl.semaphore_wait(barrier, len(partners))

    def ring(a, k, way, sub):
        slot_from = (NZ - (k - 1)) % NZ if way == 0 else k - 1
        slot_to = NZ - k if way == 0 else k
        rows = pl.ds(sub * (TILE // PARTS), TILE // PARTS)
        return remote(
            zb.at[a, slot_from, rows], zb.at[a, slot_to, rows],
            zs.at[a, k - 1, way, sub], zr.at[a, k - 1, way, sub], at_z(1 if way == 0 else -1),
        )

    def ways(k, sub):
        if k == 4:
            return [0] if sub < PARTS // 2 else [1]
        return [0, 1]

    def z_start(a):
        for sub in range(PARTS):
            for way in (0, 1):
                go(ring(a, 1, way, sub))

    def z_sub(a, k, sub):
        for way in (0, 1):
            ring(a, k, way, sub).wait_recv()
            if way in ways(k + 1, sub):
                go(ring(a, k + 1, way, sub))

    def z_last(a):
        for sub in range(PARTS):
            ring(a, 4, ways(4, sub)[0], sub).wait_recv()

    def block_at(j, d):
        return (x - j + NX) % NX, core, (y - d + NY) % NY

    def panel_peer(d, first):
        return at_x(d) if first else at_y(d)

    def p_send(b, j, d):
        ref = vp.at[b, *block_at(0 if j is None else j, 0)]
        i = 0 if j is None else 1 + j
        return remote(ref, ref, vs.at[b, i, 0, d // 2], vr.at[b, i, 0, d // 2], panel_peer(d, j is None))

    def p_pass(b, j, d):
        bx, bc, by = block_at(d, 0) if j is None else block_at(j, d)
        ref = vp.at[b, bx, bc, by, pl.ds(HALF * (d // 2), HALF)]
        i = 0 if j is None else 1 + j
        return remote(ref, ref, vs.at[b, i, 1, d // 2], vr.at[b, i, 1, d // 2], panel_peer(d, j is None))

    def p_swap(b, j, d):
        ref = vp.at[b, *block_at(j, d)]
        return remote(ref, ref, us.at[b, j, d], ur.at[b, j, d], sibling)

    def p_out(b, j):
        for d in (1, 3):
            go(p_send(b, j, d))
        go(p_swap(b, j, 0))

    def p_start(b):
        for d in (1, 3):
            go(p_send(b, None, d))
        p_out(b, 0)

    def p_first(b):
        for d in (1, 3):
            p_send(b, None, d).wait_recv()
            go(p_pass(b, None, d))
        for d in (1, 3):
            p_out(b, d)

    def p_first_far(b):
        for d in (1, 3):
            p_pass(b, None, d).wait_recv()
        p_out(b, 2)

    def p_second(b, j):
        for d in (1, 3):
            p_send(b, j, d).wait_recv()
            go(p_pass(b, j, d))
            go(p_swap(b, j, d))

    def p_second_far(b, j):
        for d in (1, 3):
            p_pass(b, j, d).wait_recv()
        go(p_swap(b, j, 2))

    def p_done(b):
        for j in range(4):
            for d in range(4):
                p_swap(b, j, d).wait_recv()

    def z_dots(a, offsets, b, total=None):
        for s in offsets:
            m = (z + s) % NZ
            v = vp[b, m // 2, m % 2].reshape(WIDTH, WIDTH)
            term = jnp.dot(zb[a, s], v, preferred_element_type=F32)
            total = term if total is None else total + term
        return total

    def o_copy(d, h):
        m = 2 * ((x + d) % NX) + h
        slot = (m - z + NZ) % NZ
        return remote(
            zb.at[OCC, slot], ob.at[h, NX - d], os_.at[d - 1, h], or_.at[d - 1, h], at_x(d)
        )

    def o_arrived(slot):
        m = (z + slot) % NZ
        d, h = (m // 2 - x + NX) % NX, m % 2

        @pl.when(d == 0)
        def _():
            ob[h, 0] = zb[OCC, slot]

        @pl.when(d != 0)
        def _():
            remote(
                zb.at[OCC, slot], ob.at[h, NX - d], os_.at[d - 1, h], or_.at[d - 1, h], at_x(d)
            ).start()

    def o_done():
        for d in (1, 2, 3):
            for h in range(2):
                o_copy(d, h).wait_recv()

    rows = lax.broadcasted_iota(jnp.int32, (8, 128), 0)
    lanes = lax.broadcasted_iota(jnp.int32, (8, 128), 1)

    def place(p, q):
        return (rows == p) & (lanes == q)

    def y_copy(p, d):
        ref = hg.at[p, core, y]
        return remote(ref, ref, ys.at[p, d - 1], yr.at[p, d - 1], at_y(d))

    def y_swap(p, j):
        ref = hg.at[p, core, (y - j + NY) % NY]
        return remote(ref, ref, ks.at[p, j], kr.at[p, j], sibling)

    def y_start(p, value):
        hg[p, core, y] = value
        for d in (2, 1, 3):
            go(y_copy(p, d))
        go(y_swap(p, 0))

    def y_done(p):
        for d in (1, 3, 2):
            y_copy(p, d).wait_recv()
            go(y_swap(p, d))

    def x_copy(p, d):
        return remote(ps.at[p, d - 1], pr.at[p, d - 1], xs.at[p, d - 1], xr.at[p, d - 1], at_x(d))

    def b_copy(d):
        return remote(bl, bx.at[NX - d], bs.at[d - 1], br.at[d - 1], at_x(d))

    def b_start():
        for d in (2, 1, 3):
            go(b_copy(d))

    def b_done():
        for d in (1, 3, 2):
            b_copy(d).wait_recv()

    def x_start(p):
        for j in range(4):
            y_swap(p, j).wait_recv()
        h0 = hg[p, 0].reshape(WIDTH, WIDTH)
        h1 = hg[p, 1].reshape(WIDTH, WIDTH)
        for d in (2, 1, 3, 0):
            part = jnp.dot(ob[0, d], h0, preferred_element_type=F32)
            part += jnp.dot(ob[1, d], h1, preferred_element_type=F32)
            pf[p, d] = part
            if d:
                ps[p, d - 1] = part.astype(BF16)
                go(x_copy(p, d))

    def x_share(q):
        mine = jnp.zeros((8, 128), F32)
        for p in range(AUX):
            total = jnp.sum(bl[p].astype(F32) * pf[q, 0], axis=0)
            for d in (1, 2, 3):
                total += jnp.sum(bx[d, p].astype(F32) * pf[q, d], axis=0)
            mine = jnp.where(place(p, q), jnp.sum(total), mine)
        return mine

    def x_done(p):
        total = pf[p, 0]
        for d in (1, 3, 2):
            x_copy(p, d).wait_recv()
            total += pr[p, d - 1].astype(F32)
        return total

    def put(q):
        return pltpu.make_async_copy(dv.at[q], dressed.at[q], outs.at[q])

    def dot_all(left, right):
        return jnp.sum(left.astype(F32) * right.astype(F32))

    def out(q, total):
        value = total.astype(BF16)
        dv[q] = value
        put(q).start()

    def d_share(q, total):
        mine = jnp.zeros((8, 128), F32)
        for p in range(AUX):
            mine = jnp.where(place(p, q), dot_all(bl[p], total), mine)
        return mine

    def q_copies(stage):
        if stage == 0:
            buffer, mine, peers, base = qs, core, [sibling], 0
        elif stage == 1:
            buffer, mine, peers, base = qa, z, [at_z(i) for i in range(1, NZ)], 1
        else:
            buffer, mine, base = qb, x * NY + y, 8
            peers = [at_xy(i // NY, i % NY) for i in range(1, NX * NY)]
        ref = buffer.at[mine]
        return buffer, mine, [
            remote(ref, ref, qss.at[base + i], qsr.at[base + i], to) for i, to in enumerate(peers)
        ]

    def q_start(stage, value):
        buffer, mine, copies = q_copies(stage)
        buffer[mine] = value
        for copy in copies:
            go(copy)

    def q_done(stage):
        buffer, _, copies = q_copies(stage)
        for copy in copies:
            copy.wait_recv()
        return jnp.sum(buffer[...], axis=0)

    shares = []
    z_start(1)
    p_start(0)
    z_start(0)
    z_start(OCC)
    p_start(1)
    p_second(0, 0)
    z_sub(1, 1, 1)
    z_start(2)
    p_first(0)
    p_first(1)
    b_start()
    p_second_far(0, 0)
    z_sub(0, 1, 1)
    z_sub(OCC, 1, 0)
    z_sub(1, 2, 1)
    z_sub(OCC, 1, 1)
    p_second(1, 0)
    z_sub(OCC, 2, 0)
    p_first_far(0)
    z_sub(2, 1, 1)
    z_sub(OCC, 2, 1)
    z_sub(1, 1, 0)
    o_arrived(1)
    p_second(0, 3)
    z_sub(2, 1, 0)
    z_sub(0, 1, 0)
    p_first_far(1)
    z_sub(OCC, 3, 0)
    z_sub(OCC, 3, 1)
    p_second(0, 1)
    z_sub(1, 2, 0)
    p_second_far(0, 3)
    o_arrived(3)
    p_second(0, 2)
    p_second_far(1, 0)
    z_sub(0, 2, 1)
    o_arrived(0)
    p_second(1, 1)
    z_sub(0, 2, 0)
    p_second(1, 2)
    z_sub(1, 3, 0)
    z_last(OCC)
    z_sub(1, 3, 1)
    p_second_far(0, 1)
    p_second(1, 3)
    o_arrived(4)
    z_sub(2, 2, 1)
    p_second_far(0, 2)
    p_done(0)
    o_arrived(2)
    o_arrived(5)
    o_arrived(7)
    p_second_far(1, 2)
    z_sub(2, 2, 0)
    z_sub(0, 3, 0)
    z_last(1)
    p_second_far(1, 1)
    y_start(1, z_dots(1, range(NZ), VIRT).astype(BF16))
    z_sub(0, 3, 1)
    p_second_far(1, 3)
    p_done(1)
    z_sub(2, 3, 1)
    z_sub(2, 3, 0)
    o_arrived(6)
    zb[3, 0] = z_dots(OCC, range(NZ), TENSOR).astype(BF16)
    z_start(3)
    z_last(0)
    y_start(0, z_dots(0, range(NZ), VIRT).astype(BF16))
    b_done()
    o_done()
    y_done(1)
    z_last(2)
    z_sub(3, 1, 0)
    y_start(2, z_dots(2, range(NZ), VIRT).astype(BF16))
    z_sub(3, 1, 1)
    x_start(1)
    z_sub(3, 2, 0)
    y_done(0)
    z_sub(3, 2, 1)
    x_start(0)
    shares.append(x_share(1))
    z_sub(3, 3, 0)
    z_sub(3, 3, 1)
    y_done(2)
    acc3 = z_dots(3, (0, 7, 1, 6, 2, 5, 3), VIRT)
    shares.append(x_share(0))
    x_start(2)
    shares.append(x_share(2))
    z_last(3)
    d3 = z_dots(3, (4,), VIRT, acc3)
    shares.append(d_share(3, d3))
    q_start(0, shares[0] + shares[1] + shares[2] + shares[3])
    q_start(1, q_done(0))
    out(3, d3)
    out(1, x_done(1))
    q_start(2, q_done(1))
    out(0, x_done(0))
    out(2, x_done(2))
    polar[...] = q_done(2)[:AUX, :AUX] / (NZ * WIDTH)
    for d in (1, 2, 3):
        for h in range(2):
            o_copy(d, h).wait_send()
    for copy in sent:
        copy.wait_send()
    for q in range(AUX):
        put(q).wait()


def on_device(tensor_tiles, tile_pairs, tile_counts, occupied, virtual):
    vmem = pl.BlockSpec(memory_space=pltpu.VMEM)
    hbm = pl.BlockSpec(memory_space=pl.ANY)
    dma = pltpu.SemaphoreType.DMA
    block = (TILE, WIDTH)
    shares, dressed = pl.pallas_call(
        kernel,
        out_shape=(
            jax.ShapeDtypeStruct((AUX, AUX), F32),
            jax.ShapeDtypeStruct((AUX, *block), BF16),
        ),
        in_specs=[hbm] * 5,
        out_specs=(vmem, hbm),
        scratch_shapes=[
            pltpu.VMEM((4, AUX, TILE, TILE), BF16),
            pltpu.SMEM((4,), jnp.int32),
            pltpu.SMEM((1,), jnp.int32),
            pltpu.VMEM((AUX, *block), BF16),
            pltpu.VMEM((NX, AUX, *block), BF16),
            pltpu.VMEM((AUX + 1, NZ, *block), BF16),
            pltpu.VMEM((2, NX, 2, NY, *block), BF16),
            pltpu.VMEM((2, NX, *block), BF16),
            pltpu.VMEM((AUX, 2, NY, *block), BF16),
            pltpu.VMEM((AUX, 3, *block), BF16),
            pltpu.VMEM((AUX, 3, *block), BF16),
            pltpu.VMEM((AUX, NX, *block), F32),
            pltpu.VMEM((AUX, *block), BF16),
            pltpu.VMEM((2, 8, 128), F32),
            pltpu.VMEM((NZ, 8, 128), F32),
            pltpu.VMEM((NX * NY, 8, 128), F32),
            dma((5, 4, 2, PARTS)), dma((5, 4, 2, PARTS)),
            dma((2, 5, 2, 2)), dma((2, 5, 2, 2)),
            dma((2, 4, 4)), dma((2, 4, 4)),
            dma((3, 2)), dma((3, 2)),
            dma((3,)), dma((3,)),
            dma((4, 3)), dma((4, 3)),
            dma((4, 4)), dma((4, 4)),
            dma((4, 3)), dma((4, 3)),
            dma((23,)), dma((23,)), dma((5,)), dma((4,)),
        ],
        compiler_params=pltpu.CompilerParams(
            collective_id=0, has_side_effects=True, vmem_limit_bytes=56 * 2**20
        ),
        cost_estimate=pl.CostEstimate(flops=4 * 2**30, bytes_accessed=2**21, transcendentals=0),
    )(tensor_tiles, tile_pairs, tile_counts, occupied, virtual)
    return shares, dressed.transpose(1, 0, 2)


def solution(mesh):
    spread = P(("row", "col", "rep"))
    return jax.shard_map(
        on_device,
        mesh=mesh,
        in_specs=(
            P(("row", "col", "rep"), None, None, None),
            spread,
            spread,
            P(("col", "rep"), "row"),
            P(("col", "rep"), "row"),
        ),
        out_specs=(P(), P(("col", "rep"), None, "row")),
        check_vma=False,
    )
```

```python
import jax
import jax.numpy as jnp
from jax import lax
from jax.experimental import pallas as pl
from jax.experimental.pallas import tpu as pltpu
from jax.sharding import PartitionSpec as P

MESH = pl.DeviceIdType.MESH
F32, BF16 = jnp.float32, jnp.bfloat16
TILE, WIDTH, AUX = 128, 512, 4
NZ, NX, NY = 8, 4, 4
HALF = TILE // 2
PARTS = 2
VIRT, TENSOR = 0, 1
OCC = 4


def kernel(
    tiles_in, pairs_in, counts_in, occ, virt, polar, dressed,
    tiles, pairs, counts, bl, bx, zb, vp, ob, hg, ps, pr, pf, wide, dv, qs, qa, qb,
    zs, zr, vs, vr, us, ur, os_, or_, bs, br, ys, yr, ks, kr, xs, xr, qss, qsr, ins, outs,
):
    z, col, y = lax.axis_index("row"), lax.axis_index("col"), lax.axis_index("rep")
    x, core = col // 2, col % 2
    sent = []

    def at_z(d):
        return ((z + d) % NZ, col, y)

    def at_x(d):
        return at_xy(d, 0)

    def at_y(d):
        return at_xy(0, d)

    def at_xy(dx, dy):
        return (z, (col + 2 * dx) % (2 * NX), (y + dy) % NY)

    sibling = (z, x * 2 + 1 - core, y)

    def remote(src, dst, send, recv, to):
        return pltpu.make_async_remote_copy(
            src_ref=src, dst_ref=dst, send_sem=send, recv_sem=recv, device_id=to, device_id_type=MESH
        )

    def go(copy):
        copy.start()
        sent.append(copy)

    loads = [
        pltpu.make_async_copy(src, dst, ins.at[i])
        for i, (src, dst) in enumerate([
            (pairs_in, pairs), (counts_in, counts), (tiles_in, tiles),
            (occ, zb.at[OCC, 0]), (virt, vp.at[VIRT, x, core, y]),
        ])
    ]
    for load in loads:
        load.start()

    barrier = pltpu.get_barrier_semaphore()
    partners = [sibling, at_z(1), at_z(-1)] + [at_xy(d, 0) for d in (1, 2, 3)] + [at_xy(0, d) for d in (1, 2, 3)]
    for to in partners:
        pl.semaphore_signal(barrier, inc=1, device_id=to, device_id_type=MESH)

    for load in loads:
        load.wait()

    live = counts[0]
    for q in range(4):
        where = jnp.int32(0)
        for t in range(1, 4):
            where = jnp.where(pairs[t] == q, jnp.int32(t), where)
        keep = where < live
        for p in range(AUX):
            tile = tiles[where, p]
            tile = jnp.where(keep, tile, jnp.zeros_like(tile))
            bl[p, :, q * TILE : (q + 1) * TILE] = tile
    for p in range(AUX):
        zb[p, 0] = bl[p]
    vp[TENSOR, x, core, y] = bl[AUX - 1]

    pl.semaphore_wait(barrier, len(partners))

    def ring(a, k, way, sub):
        slot_from = (NZ - (k - 1)) % NZ if way == 0 else k - 1
        slot_to = NZ - k if way == 0 else k
        rows = pl.ds(sub * (TILE // PARTS), TILE // PARTS)
        return remote(
            zb.at[a, slot_from, rows], zb.at[a, slot_to, rows],
            zs.at[a, k - 1, way, sub], zr.at[a, k - 1, way, sub], at_z(1 if way == 0 else -1),
        )

    def ways(k, sub):
        if k == 4:
            return [0] if sub < PARTS // 2 else [1]
        return [0, 1]

    def z_start(a):
        for sub in range(PARTS):
            for way in (0, 1):
                go(ring(a, 1, way, sub))

    def z_sub(a, k, sub):
        for way in (0, 1):
            ring(a, k, way, sub).wait_recv()
            if way in ways(k + 1, sub):
                go(ring(a, k + 1, way, sub))

    def z_last(a):
        for sub in range(PARTS):
            ring(a, 4, ways(4, sub)[0], sub).wait_recv()

    def block_at(j, d):
        return (x - j + NX) % NX, core, (y - d + NY) % NY

    def panel_peer(d, first):
        return at_x(d) if first else at_y(d)

    def p_send(b, j, d):
        ref = vp.at[b, *block_at(0 if j is None else j, 0)]
        i = 0 if j is None else 1 + j
        return remote(ref, ref, vs.at[b, i, 0, d // 2], vr.at[b, i, 0, d // 2], panel_peer(d, j is None))

    def p_pass(b, j, d):
        bx, bc, by = block_at(d, 0) if j is None else block_at(j, d)
        ref = vp.at[b, bx, bc, by, pl.ds(HALF * (d // 2), HALF)]
        i = 0 if j is None else 1 + j
        return remote(ref, ref, vs.at[b, i, 1, d // 2], vr.at[b, i, 1, d // 2], panel_peer(d, j is None))

    def p_swap(b, j, d):
        ref = vp.at[b, *block_at(j, d)]
        return remote(ref, ref, us.at[b, j, d], ur.at[b, j, d], sibling)

    def p_out(b, j):
        for d in (1, 3):
            go(p_send(b, j, d))
        go(p_swap(b, j, 0))

    def p_start(b):
        for d in (1, 3):
            go(p_send(b, None, d))
        p_out(b, 0)

    def p_first(b):
        for d in (1, 3):
            p_send(b, None, d).wait_recv()
            go(p_pass(b, None, d))
        for d in (1, 3):
            p_out(b, d)

    def p_first_far(b):
        for d in (1, 3):
            p_pass(b, None, d).wait_recv()
        p_out(b, 2)

    def p_second(b, j):
        for d in (1, 3):
            p_send(b, j, d).wait_recv()
            go(p_pass(b, j, d))
            go(p_swap(b, j, d))

    def p_second_far(b, j):
        for d in (1, 3):
            p_pass(b, j, d).wait_recv()
        go(p_swap(b, j, 2))

    def p_done(b):
        for j in range(4):
            for d in range(4):
                p_swap(b, j, d).wait_recv()

    def z_dots(a, offsets, b, total=None):
        for s in offsets:
            m = (z + s) % NZ
            v = vp[b, m // 2, m % 2].reshape(WIDTH, WIDTH)
            term = jnp.dot(zb[a, s], v, preferred_element_type=F32)
            total = term if total is None else total + term
        return total

    def o_copy(d, h):
        m = 2 * ((x + d) % NX) + h
        slot = (m - z + NZ) % NZ
        return remote(
            zb.at[OCC, slot], ob.at[h, NX - d], os_.at[d - 1, h], or_.at[d - 1, h], at_x(d)
        )

    def o_arrived(slot):
        m = (z + slot) % NZ
        d, h = (m // 2 - x + NX) % NX, m % 2

        @pl.when(d == 0)
        def _():
            ob[h, 0] = zb[OCC, slot]

        @pl.when(d != 0)
        def _():
            remote(
                zb.at[OCC, slot], ob.at[h, NX - d], os_.at[d - 1, h], or_.at[d - 1, h], at_x(d)
            ).start()

    def o_done():
        for d in (1, 2, 3):
            for h in range(2):
                o_copy(d, h).wait_recv()

    rows = lax.broadcasted_iota(jnp.int32, (8, 128), 0)
    lanes = lax.broadcasted_iota(jnp.int32, (8, 128), 1)

    def place(p, q):
        return (rows == p) & (lanes == q)

    def y_copy(p, d):
        ref = hg.at[p, core, y]
        return remote(ref, ref, ys.at[p, d - 1], yr.at[p, d - 1], at_y(d))

    def y_swap(p, j):
        ref = hg.at[p, core, (y - j + NY) % NY]
        return remote(ref, ref, ks.at[p, j], kr.at[p, j], sibling)

    def y_start(p, value):
        hg[p, core, y] = value
        for d in (2, 1, 3):
            go(y_copy(p, d))
        go(y_swap(p, 0))

    def y_done(p):
        for d in (1, 3, 2):
            y_copy(p, d).wait_recv()
            go(y_swap(p, d))

    def x_copy(p, d):
        return remote(ps.at[p, d - 1], pr.at[p, d - 1], xs.at[p, d - 1], xr.at[p, d - 1], at_x(d))

    def b_copy(d):
        return remote(bl, bx.at[NX - d], bs.at[d - 1], br.at[d - 1], at_x(d))

    def b_start():
        for d in (2, 1, 3):
            go(b_copy(d))

    def b_done():
        for d in (1, 3, 2):
            b_copy(d).wait_recv()

    def x_start(p):
        for j in range(4):
            y_swap(p, j).wait_recv()
        h0 = hg[p, 0].reshape(WIDTH, WIDTH)
        h1 = hg[p, 1].reshape(WIDTH, WIDTH)
        for d in (2, 1, 3, 0):
            part = jnp.dot(ob[0, d], h0, preferred_element_type=F32)
            part += jnp.dot(ob[1, d], h1, preferred_element_type=F32)
            pf[p, d] = part
            if d:
                ps[p, d - 1] = part.astype(BF16)
                go(x_copy(p, d))

    def x_share(q):
        mine = jnp.zeros((8, 128), F32)
        for p in range(AUX):
            total = jnp.sum(bl[p].astype(F32) * pf[q, 0], axis=0)
            for d in (1, 2, 3):
                total += jnp.sum(bx[d, p].astype(F32) * pf[q, d], axis=0)
            mine = jnp.where(place(p, q), jnp.sum(total), mine)
        return mine

    def x_done(p):
        total = pf[p, 0]
        for d in (1, 3, 2):
            x_copy(p, d).wait_recv()
            total += pr[p, d - 1].astype(F32)
        return total

    def put(q):
        return pltpu.make_async_copy(dv.at[q], dressed.at[q], outs.at[q])

    def dot_all(left, right):
        return jnp.sum(left.astype(F32) * right.astype(F32))

    def out(q, total):
        value = total.astype(BF16)
        dv[q] = value
        put(q).start()

    def d_share(total):
        return jnp.where(place(3, 3), dot_all(bl[3], total), 0.0)

    def cross_share():
        mine = jnp.zeros((8, 128), F32)
        for p in range(AUX - 1):
            mine = jnp.where(place(p, 3), dot_all(wide[3], wide[p]), mine)
        return mine

    def q_copies(stage):
        if stage == 0:
            buffer, mine, peers, base = qs, core, [sibling], 0
        elif stage == 1:
            buffer, mine, peers, base = qa, z, [at_z(i) for i in range(1, NZ)], 1
        else:
            buffer, mine, base = qb, x * NY + y, 8
            peers = [at_xy(i // NY, i % NY) for i in range(1, NX * NY)]
        ref = buffer.at[mine]
        return buffer, mine, [
            remote(ref, ref, qss.at[base + i], qsr.at[base + i], to) for i, to in enumerate(peers)
        ]

    def q_start(stage, value):
        buffer, mine, copies = q_copies(stage)
        buffer[mine] = value
        for copy in copies:
            copy.start() if stage == 2 else go(copy)

    def q_done(stage):
        buffer, _, copies = q_copies(stage)
        for copy in copies:
            copy.wait_recv()
        return jnp.sum(buffer[...], axis=0)

    def drain():
        for d in (1, 2, 3):
            for h in range(2):
                o_copy(d, h).wait_send()
        for copy in sent:
            copy.wait_send()
        for q in range(AUX):
            put(q).wait()

    shares = []
    z_start(1)
    p_start(0)
    z_start(0)
    z_start(OCC)
    p_start(1)
    p_second(0, 0)
    z_sub(1, 1, 1)
    z_start(2)
    p_first(0)
    p_first(1)
    b_start()
    p_second_far(0, 0)
    z_sub(OCC, 1, 0)
    z_sub(1, 2, 1)
    z_sub(OCC, 1, 1)
    p_second(1, 0)
    z_sub(OCC, 2, 0)
    p_first_far(0)
    z_sub(2, 1, 1)
    z_sub(OCC, 2, 1)
    z_sub(1, 1, 0)
    z_sub(0, 1, 1)
    p_second(0, 3)
    z_sub(OCC, 3, 0)
    z_sub(0, 1, 0)
    o_arrived(1)
    z_sub(2, 1, 0)
    p_first_far(1)
    z_sub(OCC, 3, 1)
    p_second(0, 1)
    z_sub(1, 2, 0)
    p_second_far(0, 3)
    o_arrived(3)
    p_second(0, 2)
    p_second_far(1, 0)
    z_sub(0, 2, 1)
    o_arrived(0)
    p_second(1, 1)
    z_sub(0, 2, 0)
    z_last(OCC)
    p_second(1, 2)
    z_sub(1, 3, 0)
    z_sub(1, 3, 1)
    p_second(1, 3)
    o_arrived(4)
    z_sub(2, 2, 1)
    p_second_far(0, 1)
    p_second_far(0, 2)
    p_done(0)
    o_arrived(2)
    o_arrived(5)
    o_arrived(7)
    p_second_far(1, 2)
    z_sub(2, 2, 0)
    z_sub(0, 3, 0)
    z_last(1)
    p_second_far(1, 1)
    wide[1] = z_dots(1, range(NZ), VIRT)
    y_start(1, wide[1].astype(BF16))
    z_sub(0, 3, 1)
    p_second_far(1, 3)
    p_done(1)
    z_sub(2, 3, 1)
    z_sub(2, 3, 0)
    o_arrived(6)
    wide[3] = z_dots(OCC, range(NZ), TENSOR)
    zb[3, 0] = wide[3].astype(BF16)
    z_start(3)
    z_last(0)
    b_done()
    wide[0] = z_dots(0, range(NZ), VIRT)
    y_start(0, wide[0].astype(BF16))
    z_last(2)
    o_done()
    y_done(1)
    z_sub(3, 1, 0)
    wide[2] = z_dots(2, range(NZ), VIRT)
    y_start(2, wide[2].astype(BF16))
    z_sub(3, 1, 1)
    x_start(1)
    z_sub(3, 2, 0)
    y_done(0)
    z_sub(3, 2, 1)
    x_start(0)
    shares.append(x_share(1))
    shares.append(cross_share())
    z_sub(3, 3, 0)
    z_sub(3, 3, 1)
    y_done(2)
    acc3 = z_dots(3, (0, 7, 1, 6, 2, 5, 3), VIRT)
    shares.append(x_share(0))
    x_start(2)
    shares.append(x_share(2))
    z_last(3)
    d3 = z_dots(3, (4,), VIRT, acc3)
    shares.append(d_share(d3))
    q_start(0, shares[0] + shares[1] + shares[2] + shares[3] + shares[4])
    q_start(1, q_done(0))
    out(1, x_done(1))
    q_start(2, q_done(1))
    out(0, x_done(0))
    out(3, d3)
    out(2, x_done(2))
    drain()
    polar[...] = q_done(2)[:AUX, :AUX] / (NZ * WIDTH)
    for copy in q_copies(2)[2]:
        copy.wait_send()


def on_device(tensor_tiles, tile_pairs, tile_counts, occupied, virtual):
    vmem = pl.BlockSpec(memory_space=pltpu.VMEM)
    hbm = pl.BlockSpec(memory_space=pl.ANY)
    dma = pltpu.SemaphoreType.DMA
    block = (TILE, WIDTH)
    shares, dressed = pl.pallas_call(
        kernel,
        out_shape=(
            jax.ShapeDtypeStruct((AUX, AUX), F32),
            jax.ShapeDtypeStruct((AUX, *block), BF16),
        ),
        in_specs=[hbm] * 5,
        out_specs=(vmem, hbm),
        scratch_shapes=[
            pltpu.VMEM((4, AUX, TILE, TILE), BF16),
            pltpu.SMEM((4,), jnp.int32),
            pltpu.SMEM((1,), jnp.int32),
            pltpu.VMEM((AUX, *block), BF16),
            pltpu.VMEM((NX, AUX, *block), BF16),
            pltpu.VMEM((AUX + 1, NZ, *block), BF16),
            pltpu.VMEM((2, NX, 2, NY, *block), BF16),
            pltpu.VMEM((2, NX, *block), BF16),
            pltpu.VMEM((AUX, 2, NY, *block), BF16),
            pltpu.VMEM((AUX, 3, *block), BF16),
            pltpu.VMEM((AUX, 3, *block), BF16),
            pltpu.VMEM((AUX, NX, *block), F32),
            pltpu.VMEM((AUX, *block), F32),
            pltpu.VMEM((AUX, *block), BF16),
            pltpu.VMEM((2, 8, 128), F32),
            pltpu.VMEM((NZ, 8, 128), F32),
            pltpu.VMEM((NX * NY, 8, 128), F32),
            dma((5, 4, 2, PARTS)), dma((5, 4, 2, PARTS)),
            dma((2, 5, 2, 2)), dma((2, 5, 2, 2)),
            dma((2, 4, 4)), dma((2, 4, 4)),
            dma((3, 2)), dma((3, 2)),
            dma((3,)), dma((3,)),
            dma((4, 3)), dma((4, 3)),
            dma((4, 4)), dma((4, 4)),
            dma((4, 3)), dma((4, 3)),
            dma((23,)), dma((23,)), dma((5,)), dma((4,)),
        ],
        compiler_params=pltpu.CompilerParams(
            collective_id=0, has_side_effects=True, vmem_limit_bytes=56 * 2**20
        ),
        cost_estimate=pl.CostEstimate(flops=4 * 2**30, bytes_accessed=2**21, transcendentals=0),
    )(tensor_tiles, tile_pairs, tile_counts, occupied, virtual)
    return shares, dressed.transpose(1, 0, 2)


def solution(mesh):
    spread = P(("row", "col", "rep"))
    return jax.shard_map(
        on_device,
        mesh=mesh,
        in_specs=(
            P(("row", "col", "rep"), None, None, None),
            spread,
            spread,
            P(("col", "rep"), "row"),
            P(("col", "rep"), "row"),
        ),
        out_specs=(P(), P(("col", "rep"), None, "row")),
        check_vma=False,
    )
```
